32 devices in a mesh: dp: 4 (over y, x), seq: 8 (over z, core).
Axes of the slice: x: 2, y: 2, z: 4, core: 2. Of those that a mesh axis runs over, the one named last changes fastest.
Arguments:
- hidden_u: bfloat16 [4096, 1024], P(('dp', 'seq')), may hold values from -6 to 6
- enc_rows: bfloat16 [12288, 1536], P(('dp', 'seq')), may hold values from -6 to 6
- enc_gain: float32 [1536], replicated, may hold values from 0.5 to 1.5
- enc_shift: float32 [1536], replicated, may hold values from -3 to 3
- proj_weight: bfloat16 [1024, 1024], P(('dp', 'seq')), may hold values from -0.1875 to 0.1875
- proj_bias: float32 [1024], replicated, may hold values from -3 to 3
- counts: int32 [4, 32], P('dp'), may hold values from 4 to 64, as said below
- offsets: int32 [4, 32], P('dp'), may hold values from 0 to 1023, as said below
- owners: int32 [4, 32], P('dp'), may hold values from 0 to 7, as said below
- dropped: int32 [4, 32], P('dp'), may hold values 0 or 1
- segments: int32 [4096], P(('dp', 'seq')), may hold values from 0 to 31, as said below
Outputs:
- grad_hidden: bfloat16 [4096, 1024], P(('dp', 'seq'))
- grad_weight: float32 [1024, 1024], P(('dp', 'seq'))
- grad_bias: float32 [1024], replicated
The draws below stay inside these ranges and needn't reach their ends.
Inputs may be any that keep to these rules, and one draw needn't show every extreme that they name: A group's counts sum to 1024. `offsets`: the images' runs of tokens lie end to end in some packing order, each token in exactly one run. `owners`: the index of seq holding the image's first token or the next one; that owner's rows of enc_rows hold its images one after another in image order from its first row, rows after them are padding. `segments`: the image whose run holds the token, consistent with offsets and counts.
All inputs are finite; a program needn't handle non-finite values. No bound on the sum of `dropped` on one device may be relied on, other than what follows from the above.
Results may differ from the reference program's by a relative error of at most 0.0058.
Values may be sent and summed in bfloat16 or wider, within the bound.
A program may use at most 64 MiB of HBM per device.

```python
import jax
import jax.numpy as jnp
from jax import lax

EW = 1536
EO = 1024
PH = 1024
TOK_DEV = 128
IMG_DEV = 4
SEQ = 1024
IMGS = 32
ROWS = 4096
ENC_CAP = 384
GROUP_ENC = 3072
ENC_ROWS = 12288
N_DP = 4
N_SEQ = 8


def image_layout(key):
    base_key = jax.random.fold_in(key, 7919)
    average_len = TOK_DEV // IMG_DEV
    lower_len = max(1, average_len // 8)
    upper_len = 2 * average_len

    def one_group(group_key):
        sizes_now = jnp.full((IMGS,), average_len, jnp.int32)
        for turn in range(3):
            order_key, pick_key = jax.random.split(jax.random.fold_in(group_key, 10 + turn))
            order = jax.random.permutation(order_key, IMGS)
            first_half = order[0::2]
            second_half = order[1::2]
            summed = sizes_now[first_half] + sizes_now[second_half]
            lowest = jnp.maximum(lower_len, summed - upper_len)
            highest = jnp.minimum(upper_len, summed - lower_len)
            picked = jax.random.randint(pick_key, (IMGS // 2,), lowest, highest + 1).astype(jnp.int32)
            sizes_now = sizes_now.at[first_half].set(picked).at[second_half].set((summed - picked).astype(jnp.int32))
        packing = jax.random.permutation(jax.random.fold_in(group_key, 20), IMGS).astype(jnp.int32)
        packed_sizes = sizes_now[packing]
        run_ends = jnp.cumsum(packed_sizes).astype(jnp.int32)
        run_starts = (run_ends - packed_sizes).astype(jnp.int32)
        starts = jnp.zeros((IMGS,), jnp.int32).at[packing].set(run_starts)
        position = jnp.arange(SEQ, dtype=jnp.int32)
        rank = jnp.sum((position[:, None] >= run_ends[None, :]).astype(jnp.int32), axis=1)
        seg_ids = packing[rank].astype(jnp.int32)
        start_shard = (starts // TOK_DEV).astype(jnp.int32)
        moved = jax.random.randint(jax.random.fold_in(group_key, 30), (IMGS,), 0, 2).astype(jnp.int32)
        holder = jnp.where(start_shard == N_SEQ - 1, start_shard, start_shard + moved).astype(jnp.int32)
        return (sizes_now, starts, holder, seg_ids)
    group_keys = jax.vmap(lambda number: jax.random.fold_in(base_key, number))(jnp.arange(N_DP))
    return jax.vmap(one_group)(group_keys)


def draw_counts(key, part):
    return image_layout(key)[0].astype(jnp.int32)


def draw_offsets(key, part):
    return image_layout(key)[1].astype(jnp.int32)


def draw_owners(key, part):
    return image_layout(key)[2].astype(jnp.int32)


def draw_segments(key, part):
    return image_layout(key)[3].reshape(-1).astype(jnp.int32)


def plant(values, key, low, high):
    longest = values.shape.index(max(values.shape))
    spots = []
    for shift in (0, 1):
        where = [jax.random.randint(jax.random.fold_in(key, axis), (), 0, length) for axis, length in enumerate(values.shape)]
        where[longest] = (where[longest] + shift) % values.shape[longest]
        spots.append(tuple(where))
    return values.at[spots[0]].set(low).at[spots[1]].set(high)


def with_spikes(drawn, key, source, target, blocks, factor):
    def block_of(axis_at):
        return (jnp.arange(drawn.shape[axis_at]) // (drawn.shape[axis_at] // blocks)).reshape((-1,) + (1,) * (drawn.ndim - 1 - axis_at))

    near = jax.random.permutation(key, blocks)[block_of(target)]
    second = (block_of(target) + blocks // 2) % blocks
    return jnp.where((block_of(source) == near) | (block_of(source) == second), factor * drawn, drawn)


def block_scale(stream_key, dims, cuts, least, largest):
    loudness = 1.0
    for dim, parts in cuts:
        draws = jax.random.uniform(jax.random.fold_in(jax.random.fold_in(stream_key, 6), dim), (parts,), jnp.float32, least / len(cuts), largest / len(cuts))
        loudness = loudness * jnp.repeat(jnp.exp(draws), dims[dim] // parts).reshape((-1,) + (1,) * (len(dims) - 1 - dim))
    return loudness


def bell_draw(rng, dims, scale, reach, cuts=(), kind=jnp.bfloat16):
    entries = jax.random.normal(rng, dims, jnp.float32) * scale
    if len(cuts) > 0:
        entries = block_scale(rng, dims, cuts, -0.22, 0.18) * entries
    return jnp.clip(entries, min=-reach, max=reach).astype(kind)


def noise_with(rng, extent, scale, most, cuts, heavy, held_as=jnp.bfloat16):
    drawn = scale * jax.random.normal(rng, extent, jnp.float32)
    if cuts:
        drawn = drawn * block_scale(rng, extent, cuts, -0.22, 0.18)
    return jnp.clip(with_spikes(drawn, jax.random.fold_in(rng, 3), *heavy), -most, most).astype(held_as)


def setup_inputs(seed: int = 0) -> dict:
    key_list = jax.random.split(jax.random.key(seed), 12)
    hidden_u = noise_with(key_list[0], (ROWS, PH), 1.0, 6.0, ((0, 32),), (0, 1, 32, 2.75))
    enc_rows = bell_draw(key_list[1], (ENC_ROWS, EW), 1.0, 6.0, ((0, 32),))
    enc_gain = jnp.clip(1.0 + 0.1 * jax.random.normal(key_list[2], (EW,), jnp.float32), 0.5, 1.5)
    enc_shift = bell_draw(key_list[3], (EW,), 0.5, 3.0, (), jnp.float32)
    proj_weight = bell_draw(key_list[4], (PH, EO), PH ** -0.5, 0.1875, ((0, 32),))
    proj_bias = bell_draw(key_list[5], (EO,), 0.5, 3.0, (), jnp.float32)
    counts = draw_counts(jax.random.fold_in(key_list[11], 71), 0)
    offsets = draw_offsets(jax.random.fold_in(key_list[11], 71), 0)
    owners = draw_owners(jax.random.fold_in(key_list[11], 71), 0)
    dropped = plant((jax.random.randint(key_list[9], (N_DP, IMGS), 0, 5) < 1).astype(jnp.int32), jax.random.fold_in(key_list[9], 1), 0, 1)
    segments = draw_segments(jax.random.fold_in(key_list[11], 71), 0)
    return dict(hidden_u=hidden_u, enc_rows=enc_rows, enc_gain=enc_gain, enc_shift=enc_shift, proj_weight=proj_weight, proj_bias=proj_bias, counts=counts, offsets=offsets, owners=owners, dropped=dropped, segments=segments)


NORM_EPS = 1e-06
LENGTH_EPS = 1e-06
LOSS_SCALE = 1024.0
DROP_WEIGHT = 0.5

def layer_norm(values, enc_gain, enc_shift):
    widened = values.astype(jnp.float32)
    center = widened - lax.optimization_barrier(jnp.mean(widened, axis=-1, keepdims=True))
    spread = lax.optimization_barrier(jnp.mean(center * center, axis=-1, keepdims=True))
    return (center * lax.rsqrt(spread + NORM_EPS) * enc_gain + enc_shift).astype(jnp.bfloat16)

def align_grad(projected, target, weight_tok):
    widened = target.astype(jnp.float32)
    inv_proj = lax.rsqrt(lax.optimization_barrier(jnp.sum(projected * projected, axis=1, keepdims=True)) + LENGTH_EPS)
    inv_target = lax.rsqrt(lax.optimization_barrier(jnp.sum(widened * widened, axis=1, keepdims=True)) + LENGTH_EPS)
    cosine = lax.optimization_barrier(jnp.sum(projected * widened, axis=1, keepdims=True)) * inv_proj * inv_target
    factor = -LOSS_SCALE * weight_tok[:, None]
    return (factor * (widened * inv_proj * inv_target - cosine * projected * inv_proj * inv_proj)).astype(jnp.bfloat16)

def reference(hidden_u, enc_rows, enc_gain, enc_shift, proj_weight, proj_bias, counts, offsets, owners, dropped, segments):
    index = jnp.arange(IMGS, dtype=jnp.int32)
    position = jnp.arange(SEQ, dtype=jnp.int32)
    grad_weight = jnp.zeros((PH, EO), jnp.float32)
    grad_bias = jnp.zeros((EO,), jnp.float32)
    pieces = []
    for group in range(N_DP):
        tokens_u = hidden_u[group * SEQ:(group + 1) * SEQ]
        group_rows = enc_rows[group * GROUP_ENC:(group + 1) * GROUP_ENC]
        group_seg = segments[group * SEQ:(group + 1) * SEQ].astype(jnp.int32)
        image_count = counts[group].astype(jnp.int32)
        image_start = offsets[group].astype(jnp.int32)
        image_owner = owners[group].astype(jnp.int32)
        image_drop = dropped[group].astype(jnp.int32)
        earlier = (image_owner[:, None] == image_owner[None, :]) & (index[None, :] < index[:, None])
        base_row = lax.optimization_barrier(jnp.sum(jnp.where(earlier, image_count[None, :], 0), axis=1)).astype(jnp.int32)
        row_index = (image_owner[group_seg] * ENC_CAP + base_row[group_seg] + position - image_start[group_seg]).astype(jnp.int32)
        target = layer_norm(group_rows[row_index], enc_gain, enc_shift)[:, :EO]
        count_tok = image_count[group_seg].astype(jnp.float32)
        weight_tok = jnp.where(image_drop[group_seg] == 1, DROP_WEIGHT, 1.0) / count_tok
        projected = jnp.dot(tokens_u, proj_weight, preferred_element_type=jnp.float32) + proj_bias
        grad_proj = align_grad(projected, target, weight_tok)
        pieces.append(jnp.dot(grad_proj, proj_weight.T, preferred_element_type=jnp.float32).astype(jnp.bfloat16))
        grad_weight = grad_weight + jnp.dot(tokens_u.T, grad_proj, preferred_element_type=jnp.float32)
        grad_bias = grad_bias + lax.optimization_barrier(jnp.sum(grad_proj.astype(jnp.float32), axis=0))
    return (jnp.concatenate(pieces, axis=0), grad_weight, grad_bias)
```

```python
import functools

import jax
import jax.numpy as jnp
from jax import lax
from jax.experimental import pallas as pl
from jax.experimental.pallas import tpu as pltpu
from jax.sharding import PartitionSpec as P

NORM_EPS = 1e-06
LENGTH_EPS = 1e-06
LOSS_SCALE = 1024.0
DROP_WEIGHT = 0.5


def passed_along(value, axis, steps):
    count = lax.axis_size(axis)
    first, last = (max(0, -steps), min(count, count - steps))
    return lax.ppermute(value, axis, [(source, source + steps) for source in range(first, last)])


def layer_norm(values, enc_gain, enc_shift):
    widened = values.astype(jnp.float32)
    center = widened - jnp.mean(widened, axis=-1, keepdims=True)
    spread = jnp.mean(center * center, axis=-1, keepdims=True)
    return (center * lax.rsqrt(spread + NORM_EPS) * enc_gain + enc_shift).astype(jnp.bfloat16)


def align_grad(projected, target, weight_tok):
    widened = target.astype(jnp.float32)
    inv_proj = lax.rsqrt(jnp.sum(projected * projected, axis=1, keepdims=True) + LENGTH_EPS)
    inv_target = lax.rsqrt(jnp.sum(widened * widened, axis=1, keepdims=True) + LENGTH_EPS)
    cosine = jnp.sum(projected * widened, axis=1, keepdims=True) * inv_proj * inv_target
    factor = -LOSS_SCALE * weight_tok[:, None]
    return (
        factor * (widened * inv_proj * inv_target - cosine * projected * inv_proj * inv_proj)
    ).astype(jnp.bfloat16)


def body(
    hidden_u,
    enc_rows,
    enc_gain,
    enc_shift,
    proj_weight,
    proj_bias,
    counts,
    offsets,
    owners,
    dropped,
    segments,
):
    tok_rows = hidden_u.shape[0]
    spill_len = tok_rows // 2
    out_width = proj_weight.shape[1]
    seq_index = lax.axis_index("seq")
    image_count = counts[0]
    image_start = offsets[0]
    image_owner = owners[0]
    image_drop = dropped[0]
    images = image_count.shape[0]
    index = jnp.arange(images, dtype=jnp.int32)
    earlier = (image_owner[:, None] == image_owner[None, :]) & (index[None, :] < index[:, None])
    base_row = jnp.sum(jnp.where(earlier, image_count[None, :], 0), axis=1)
    source = layer_norm(enc_rows, enc_gain, enc_shift)[:, :out_width]

    def select(target_shard, row_total):
        places = target_shard * tok_rows + jnp.arange(row_total, dtype=jnp.int32)
        inside = (places[:, None] >= image_start[None, :]) & (
            places[:, None] < (image_start + image_count)[None, :]
        )
        from_here = inside & (image_owner == seq_index)[None, :]
        row_index = jnp.sum(
            jnp.where(from_here, (base_row - image_start)[None, :] + places[:, None], 0), axis=1
        )
        present = jnp.any(from_here, axis=1)
        picked = jnp.take(source, jnp.clip(row_index, 0, source.shape[0] - 1), axis=0)
        return jnp.where(present[:, None], picked, jnp.zeros_like(picked))

    from_next = passed_along(select(seq_index - 1, tok_rows), "seq", -1)
    from_previous = passed_along(select(seq_index + 1, spill_len), "seq", 1)
    padded_spill = jnp.concatenate(
        [
            from_previous,
            jnp.zeros((tok_rows - spill_len, from_previous.shape[1]), from_previous.dtype),
        ],
        axis=0,
    )
    target = from_next + select(seq_index, tok_rows) + padded_spill
    same_image = segments[:, None] == index[None, :]
    count_tok = jnp.sum(jnp.where(same_image, image_count[None, :], 0), axis=1).astype(jnp.float32)
    drop_tok = jnp.sum(jnp.where(same_image, image_drop[None, :], 0), axis=1)
    weight_tok = jnp.where(drop_tok == 1, DROP_WEIGHT, 1.0) / count_tok
    group_weight = lax.all_gather(proj_weight, "seq", axis=0, tiled=True)
    columns = hidden_u
    projected = (
        jnp.dot(
            columns,
            lax.all_gather(group_weight, "dp", axis=0, tiled=True),
            preferred_element_type=jnp.float32,
        )
        + proj_bias
    )
    grad_proj = align_grad(projected, target, weight_tok)
    grad_hidden = lax.dot_general(
        grad_proj,
        lax.all_gather(group_weight, "dp", axis=0, tiled=True),
        (((1,), (1,)), ((), ())),
        preferred_element_type=jnp.float32,
    ).astype(jnp.bfloat16)
    columns = hidden_u
    group_grad = lax.psum_scatter(
        lax.dot_general(
            columns, grad_proj, (((0,), (0,)), ((), ())), preferred_element_type=jnp.float32
        ),
        "dp",
        scatter_dimension=0,
        tiled=True,
    )
    grad_weight = lax.psum_scatter(group_grad, "seq", scatter_dimension=0, tiled=True)
    grad_bias = lax.psum(jnp.sum(grad_proj, axis=0, dtype=jnp.float32), ("dp", "seq"))
    return (grad_hidden, grad_weight, grad_bias)


def fused_kernel(
    n_dp,
    n_seq,
    hidden_ref,
    enc_ref,
    gain_ref,
    shift_ref,
    weight_ref,
    bias_ref,
    counts_ref,
    offsets_ref,
    owners_ref,
    dropped_ref,
    grad_hidden_ref,
    grad_weight_ref,
    grad_bias_ref,
    layer,
    source,
    hidden_t,
    to_prev,
    to_next,
    from_next,
    from_prev,
    target,
    grad_proj,
    partial,
    pair_out,
    pair_in,
    dp_out,
    dp_in,
    own_sum,
    z_out,
    z_in,
    bias_own,
    bias_pair,
    bias_mid,
    bias_dp,
    bias_last,
    bias_z,
    send_sem,
    recv_sem,
):
    f32, bf16 = jnp.float32, jnp.bfloat16
    n_z = n_seq // 2
    tok_rows, depth = hidden_ref.shape
    rows, out_width = weight_ref.shape
    enc_cap = enc_ref.shape[0]
    spill_len = to_next.shape[0]
    images = counts_ref.shape[1]
    dp = lax.axis_index("dp")
    seq = lax.axis_index("seq")
    z, core = seq // 2, seq % 2
    mate_seq = z * 2 + 1 - core
    mate = (dp, mate_seq)
    used = []

    def copy(src, dst, device):
        slot = len(used)
        used.append(slot)
        return pltpu.make_async_remote_copy(
            src_ref=src,
            dst_ref=dst,
            send_sem=send_sem.at[slot],
            recv_sem=recv_sem.at[slot],
            device_id=device,
            device_id_type=pl.DeviceIdType.MESH,
        )

    def dp_at(k):
        return lax.rem(dp + (k + n_dp), n_dp)

    def z_at(k):
        return lax.rem(z + (k + n_z), n_z)

    def layer_rows(dp_index, z_index, core_index):
        start = ((dp_index * n_z + z_index) * 2 + core_index) * rows
        return layer.at[pl.ds(pl.multiple_of(start, rows), rows)]

    barrier = pltpu.get_barrier_semaphore()
    for k in range(1, n_seq):
        pl.semaphore_signal(
            barrier,
            inc=1,
            device_id=(dp, lax.rem(seq + k, n_seq)),
            device_id_type=pl.DeviceIdType.MESH,
        )
    for k in range(1, n_dp):
        pl.semaphore_signal(
            barrier, inc=1, device_id=(dp_at(k), seq), device_id_type=pl.DeviceIdType.MESH
        )
    own_rows = layer_rows(dp, z, core)
    own_rows[...] = weight_ref[...]
    pl.semaphore_wait(barrier, n_seq + n_dp - 2)

    in_flight = []

    def start(src, dst, device):
        one = copy(src, dst, device)
        one.start()
        in_flight.append(one)
        return one

    z_copies = {}
    dp_copies = {}
    mate_copies = []

    def spread(kz):
        block = layer_rows(dp, z_at(-kz), core)
        for k in range(1, n_dp):
            dp_copies[kz, k] = start(block, block, (dp_at(k), seq))
        mate_copies.append(start(block, block, mate))

    for kz in range(1, n_z):
        z_copies[kz] = start(own_rows, own_rows, (dp, z_at(kz) * 2 + core))
    spread(0)

    gain = gain_ref[:, :]
    shift = shift_ref[:, :]
    step = 32 if enc_cap % 32 == 0 else enc_cap

    def norm_step(i, carry):
        at = pl.ds(pl.multiple_of(i * step, step), step)
        source[at] = layer_norm(enc_ref[at], gain, shift)[:, :out_width]
        return carry

    lax.fori_loop(0, enc_cap // step, norm_step, 0)

    count = counts_ref[...].astype(f32)
    first = offsets_ref[...].astype(f32)
    owner = owners_ref[...].astype(f32)
    drop = dropped_ref[...].astype(f32)
    down = lax.broadcasted_iota(jnp.int32, (images, images), 0)
    across = lax.broadcasted_iota(jnp.int32, (images, images), 1)

    def as_column(row):
        return jnp.sum(jnp.where(down == across, row, 0.0), axis=1, keepdims=True)

    earlier = (as_column(owner) == owner) & (down < across)
    base = jnp.sum(jnp.where(earlier, as_column(count), 0.0), axis=0, keepdims=True)

    def inside_of(shard, row_total):
        places = (
            shard * tok_rows + lax.broadcasted_iota(jnp.int32, (row_total, 1), 0)
        ).astype(f32)
        return places, (places >= first) & (places < first + count)

    def select(shard, row_total):
        places, inside = inside_of(shard, row_total)
        from_here = inside & (owner == seq.astype(f32))
        row_index = jnp.sum(
            jnp.where(from_here, base - first + places + 1.0, 0.0), axis=1, keepdims=True
        )
        lanes = lax.broadcasted_iota(jnp.int32, (row_total, enc_cap), 1).astype(f32)
        chosen = jnp.where(lanes + 1.0 == row_index, 1.0, 0.0).astype(bf16)
        return jnp.dot(chosen, source[...], preferred_element_type=f32)

    to_prev[...] = select(seq - 1, tok_rows).astype(bf16)
    prev_copy = copy(to_prev, from_next, (dp, jnp.maximum(seq - 1, 0)))

    @pl.when(seq > 0)
    def _():
        prev_copy.start()

    to_next[...] = select(seq + 1, spill_len).astype(bf16)
    next_copy = copy(to_next, from_prev, (dp, jnp.minimum(seq + 1, n_seq - 1)))

    @pl.when(seq < n_seq - 1)
    def _():
        next_copy.start()

    for kz in range(1, n_z):
        z_copies[kz].wait_recv()
        spread(kz)

    target[...] = select(seq, tok_rows)
    hidden_t[...] = hidden_ref[...].T

    for kz in range(n_z):
        for k in range(1, n_dp):
            dp_copies[kz, k].wait_recv()
            block = layer_rows(dp_at(-k), z_at(-kz), core)
            mate_copies.append(start(block, block, mate))

    @pl.when(seq < n_seq - 1)
    def _():
        prev_copy.wait_recv()
        target[...] += from_next[...].astype(f32)

    @pl.when(seq > 0)
    def _():
        next_copy.wait_recv()
        target[:spill_len] += from_prev[...].astype(f32)

    for one in mate_copies:
        one.wait_recv()

    _, inside = inside_of(seq, tok_rows)
    count_tok = jnp.sum(jnp.where(inside, count, 0.0), axis=1, keepdims=True)
    drop_tok = jnp.sum(jnp.where(inside, drop, 0.0), axis=1, keepdims=True)
    weight_tok = jnp.where(drop_tok == 1.0, DROP_WEIGHT, 1.0) / count_tok
    projected = jnp.dot(hidden_ref[...], layer[...], preferred_element_type=f32) + bias_ref[...]
    widened = target[...]
    inv_proj = lax.rsqrt(jnp.sum(projected * projected, axis=1, keepdims=True) + LENGTH_EPS)
    inv_target = lax.rsqrt(jnp.sum(widened * widened, axis=1, keepdims=True) + LENGTH_EPS)
    cosine = jnp.sum(projected * widened, axis=1, keepdims=True) * inv_proj * inv_target
    factor = -LOSS_SCALE * weight_tok
    grad_proj[...] = (
        factor * (widened * inv_proj * inv_target - cosine * projected * inv_proj * inv_proj)
    ).astype(bf16)

    bias_own[...] = jnp.sum(grad_proj[...].astype(f32), axis=0, keepdims=True)
    bias_mate = start(bias_own, bias_pair, mate)

    chunk = depth // n_dp

    def partial_step(i, carry):
        at = pl.ds(pl.multiple_of(i * chunk, chunk), chunk)
        partial[at] = jnp.dot(hidden_t[at], grad_proj[...], preferred_element_type=f32)
        return carry

    lax.fori_loop(0, n_dp, partial_step, 0)

    def partial_rows(dp_index, z_index, core_index):
        begin = ((dp_index * n_z + z_index) * 2 + core_index) * rows
        return partial[pl.ds(pl.multiple_of(begin, rows), rows)]

    order = list(range(1, n_z)) + [0]
    pair_copies = {}
    for kz in order:
        for k in range(n_dp):
            pair_out[kz, k] = partial_rows(dp_at(k), z_at(kz), 1 - core).astype(bf16)
        pair_copies[kz] = start(pair_out.at[kz], pair_in.at[kz], mate)

    bias_mate.wait_recv()
    bias_mid[...] = bias_own[...] + bias_pair[...]
    bias_dp[pl.ds(dp, 1)] = bias_mid[...][None]
    bias_dp_copies = [
        start(bias_mid, bias_dp.at[dp], (dp_at(k), seq)) for k in range(1, n_dp)
    ]

    sum_copies = {}
    for kz in order:
        pair_copies[kz].wait_recv()
        for k in range(1, n_dp):
            total = partial_rows(dp_at(k), z_at(kz), core) + pair_in[kz, k].astype(f32)
            dp_out[kz, k - 1] = total.astype(bf16)
            sum_copies[kz, k] = start(
                dp_out.at[kz, k - 1], dp_in.at[kz, k - 1], (dp_at(k), seq)
            )
        own_sum[kz] = partial_rows(dp, z_at(kz), core) + pair_in[kz, 0].astype(f32)

    for one in bias_dp_copies:
        one.wait_recv()
    summed = bias_dp[0]
    for k in range(1, n_dp):
        summed += bias_dp[k]
    bias_last[...] = summed
    bias_z[pl.ds(z, 1)] = summed[None]
    bias_z_copies = [
        start(bias_last, bias_z.at[z], (dp, z_at(kz) * 2 + core)) for kz in range(1, n_z)
    ]

    grad_hidden_ref[...] = lax.dot_general(
        grad_proj[...], layer[...], (((1,), (1,)), ((), ())), preferred_element_type=f32
    ).astype(bf16)

    last_copies = []
    for kz in order:
        total = own_sum[kz]
        for k in range(1, n_dp):
            sum_copies[kz, k].wait_recv()
            total += dp_in[kz, k - 1].astype(f32)
        if kz:
            z_out[kz - 1] = total.astype(bf16)
            last_copies.append(
                start(z_out.at[kz - 1], z_in.at[kz - 1], (dp, z_at(kz) * 2 + core))
            )
        else:
            own_sum[0] = total

    for one in bias_z_copies:
        one.wait_recv()
    summed = bias_z[0]
    for kz in range(1, n_z):
        summed += bias_z[kz]
    grad_bias_ref[...] = summed

    total = own_sum[0]
    for at, one in enumerate(last_copies):
        one.wait_recv()
        total += z_in[at].astype(f32)
    grad_weight_ref[...] = total

    for one in in_flight:
        one.wait_send()

    @pl.when(seq > 0)
    def _():
        prev_copy.wait_send()

    @pl.when(seq < n_seq - 1)
    def _():
        next_copy.wait_send()


def fused_body(
    hidden_u,
    enc_rows,
    enc_gain,
    enc_shift,
    proj_weight,
    proj_bias,
    counts,
    offsets,
    owners,
    dropped,
    segments,
):
    n_dp, n_seq = lax.axis_size("dp"), lax.axis_size("seq")
    n_z = n_seq // 2
    tok_rows, depth = hidden_u.shape
    rows, out_width = proj_weight.shape
    enc_cap = enc_rows.shape[0]
    spill_len = tok_rows // 2
    f32, bf16 = jnp.float32, jnp.bfloat16
    copies = 3 * n_z * n_dp + 2 * n_z + n_z * n_dp + 4 * n_z + 2 * n_dp + 8
    vmem = pl.BlockSpec(memory_space=pltpu.VMEM)
    grad_hidden, grad_weight, grad_bias = pl.pallas_call(
        functools.partial(fused_kernel, n_dp, n_seq),
        out_shape=(
            jax.ShapeDtypeStruct((tok_rows, depth), bf16),
            jax.ShapeDtypeStruct((rows, out_width), f32),
            jax.ShapeDtypeStruct((1, out_width), f32),
        ),
        in_specs=[vmem] * 10,
        out_specs=(vmem, vmem, vmem),
        scratch_shapes=[
            pltpu.VMEM((depth, out_width), bf16),
            pltpu.VMEM((enc_cap, out_width), bf16),
            pltpu.VMEM((depth, tok_rows), bf16),
            pltpu.VMEM((tok_rows, out_width), bf16),
            pltpu.VMEM((spill_len, out_width), bf16),
            pltpu.VMEM((tok_rows, out_width), bf16),
            pltpu.VMEM((spill_len, out_width), bf16),
            pltpu.VMEM((tok_rows, out_width), f32),
            pltpu.VMEM((tok_rows, out_width), bf16),
            pltpu.VMEM((depth, out_width), f32),
            pltpu.VMEM((n_z, n_dp, rows, out_width), bf16),
            pltpu.VMEM((n_z, n_dp, rows, out_width), bf16),
            pltpu.VMEM((n_z, n_dp - 1, rows, out_width), bf16),
            pltpu.VMEM((n_z, n_dp - 1, rows, out_width), bf16),
            pltpu.VMEM((n_z, rows, out_width), f32),
            pltpu.VMEM((n_z - 1, rows, out_width), bf16),
            pltpu.VMEM((n_z - 1, rows, out_width), bf16),
            pltpu.VMEM((1, out_width), f32),
            pltpu.VMEM((1, out_width), f32),
            pltpu.VMEM((1, out_width), f32),
            pltpu.VMEM((n_dp, 1, out_width), f32),
            pltpu.VMEM((1, out_width), f32),
            pltpu.VMEM((n_z, 1, out_width), f32),
            pltpu.SemaphoreType.DMA((copies,)),
            pltpu.SemaphoreType.DMA((copies,)),
        ],
        compiler_params=pltpu.CompilerParams(
            collective_id=0, has_side_effects=True, vmem_limit_bytes=48 * 1024 * 1024
        ),
    )(
        hidden_u,
        enc_rows,
        enc_gain[None, :],
        enc_shift[None, :],
        proj_weight,
        proj_bias[None, :],
        counts,
        offsets,
        owners,
        dropped,
    )
    return grad_hidden, grad_weight, grad_bias[0]


def either(*arrays):
    rows, tokens = arrays[4].shape[0], arrays[0].shape[0]
    n_dp, n_seq = lax.axis_size("dp"), lax.axis_size("seq")
    whole_tiles = rows % 16 == 0 and tokens % 32 == 0
    if whole_tiles and n_seq % 2 == 0 and n_seq >= 4 and n_dp >= 2:
        return fused_body(*arrays)
    return body(*arrays)


def solution(mesh):
    placed = (
        P(("dp", "seq"), None),
        P(("dp", "seq"), None),
        P(),
        P(),
        P(("dp", "seq"), None),
        P(),
        P("dp", None),
        P("dp", None),
        P("dp", None),
        P("dp", None),
        P(("dp", "seq")),
    )
    return jax.shard_map(
        either,
        mesh=mesh,
        in_specs=placed,
        out_specs=(P(("dp", "seq"), None), P(("dp", "seq"), None), P()),
        check_vma=False,
    )
```

```python
import functools

import jax
import jax.numpy as jnp
from jax import lax
from jax.experimental import pallas as pl
from jax.experimental.pallas import tpu as pltpu
from jax.sharding import PartitionSpec as P

NORM_EPS = 1e-06
LENGTH_EPS = 1e-06
LOSS_SCALE = 1024.0
DROP_WEIGHT = 0.5


def passed_along(value, axis, steps):
    count = lax.axis_size(axis)
    first, last = (max(0, -steps), min(count, count - steps))
    return lax.ppermute(value, axis, [(source, source + steps) for source in range(first, last)])


def layer_norm(values, enc_gain, enc_shift):
    widened = values.astype(jnp.float32)
    center = widened - jnp.mean(widened, axis=-1, keepdims=True)
    spread = jnp.mean(center * center, axis=-1, keepdims=True)
    return (center * lax.rsqrt(spread + NORM_EPS) * enc_gain + enc_shift).astype(jnp.bfloat16)


def align_grad(projected, target, weight_tok):
    widened = target.astype(jnp.float32)
    inv_proj = lax.rsqrt(jnp.sum(projected * projected, axis=1, keepdims=True) + LENGTH_EPS)
    inv_target = lax.rsqrt(jnp.sum(widened * widened, axis=1, keepdims=True) + LENGTH_EPS)
    cosine = jnp.sum(projected * widened, axis=1, keepdims=True) * inv_proj * inv_target
    factor = -LOSS_SCALE * weight_tok[:, None]
    return (
        factor * (widened * inv_proj * inv_target - cosine * projected * inv_proj * inv_proj)
    ).astype(jnp.bfloat16)


def body(
    hidden_u,
    enc_rows,
    enc_gain,
    enc_shift,
    proj_weight,
    proj_bias,
    counts,
    offsets,
    owners,
    dropped,
    segments,
):
    tok_rows = hidden_u.shape[0]
    spill_len = tok_rows // 2
    out_width = proj_weight.shape[1]
    seq_index = lax.axis_index("seq")
    image_count = counts[0]
    image_start = offsets[0]
    image_owner = owners[0]
    image_drop = dropped[0]
    images = image_count.shape[0]
    index = jnp.arange(images, dtype=jnp.int32)
    earlier = (image_owner[:, None] == image_owner[None, :]) & (index[None, :] < index[:, None])
    base_row = jnp.sum(jnp.where(earlier, image_count[None, :], 0), axis=1)
    source = layer_norm(enc_rows, enc_gain, enc_shift)[:, :out_width]

    def select(target_shard, row_total):
        places = target_shard * tok_rows + jnp.arange(row_total, dtype=jnp.int32)
        inside = (places[:, None] >= image_start[None, :]) & (
            places[:, None] < (image_start + image_count)[None, :]
        )
        from_here = inside & (image_owner == seq_index)[None, :]
        row_index = jnp.sum(
            jnp.where(from_here, (base_row - image_start)[None, :] + places[:, None], 0), axis=1
        )
        present = jnp.any(from_here, axis=1)
        picked = jnp.take(source, jnp.clip(row_index, 0, source.shape[0] - 1), axis=0)
        return jnp.where(present[:, None], picked, jnp.zeros_like(picked))

    from_next = passed_along(select(seq_index - 1, tok_rows), "seq", -1)
    from_previous = passed_along(select(seq_index + 1, spill_len), "seq", 1)
    padded_spill = jnp.concatenate(
        [
            from_previous,
            jnp.zeros((tok_rows - spill_len, from_previous.shape[1]), from_previous.dtype),
        ],
        axis=0,
    )
    target = from_next + select(seq_index, tok_rows) + padded_spill
    same_image = segments[:, None] == index[None, :]
    count_tok = jnp.sum(jnp.where(same_image, image_count[None, :], 0), axis=1).astype(jnp.float32)
    drop_tok = jnp.sum(jnp.where(same_image, image_drop[None, :], 0), axis=1)
    weight_tok = jnp.where(drop_tok == 1, DROP_WEIGHT, 1.0) / count_tok
    group_weight = lax.all_gather(proj_weight, "seq", axis=0, tiled=True)
    columns = hidden_u
    projected = (
        jnp.dot(
            columns,
            lax.all_gather(group_weight, "dp", axis=0, tiled=True),
            preferred_element_type=jnp.float32,
        )
        + proj_bias
    )
    grad_proj = align_grad(projected, target, weight_tok)
    grad_hidden = lax.dot_general(
        grad_proj,
        lax.all_gather(group_weight, "dp", axis=0, tiled=True),
        (((1,), (1,)), ((), ())),
        preferred_element_type=jnp.float32,
    ).astype(jnp.bfloat16)
    columns = hidden_u
    group_grad = lax.psum_scatter(
        lax.dot_general(
            columns, grad_proj, (((0,), (0,)), ((), ())), preferred_element_type=jnp.float32
        ),
        "dp",
        scatter_dimension=0,
        tiled=True,
    )
    grad_weight = lax.psum_scatter(group_grad, "seq", scatter_dimension=0, tiled=True)
    grad_bias = lax.psum(jnp.sum(grad_proj, axis=0, dtype=jnp.float32), ("dp", "seq"))
    return (grad_hidden, grad_weight, grad_bias)


def fused_kernel(
    n_dp,
    n_seq,
    hidden_hbm,
    enc_hbm,
    gain_hbm,
    shift_hbm,
    weight_hbm,
    bias_hbm,
    counts_hbm,
    offsets_hbm,
    owners_hbm,
    dropped_hbm,
    grad_hidden_ref,
    grad_weight_ref,
    grad_bias_ref,
    layer,
    source,
    hidden_t,
    to_prev,
    to_next,
    from_next,
    from_prev,
    target,
    grad_proj,
    partial,
    pair_out,
    pair_in,
    dp_out,
    dp_in,
    own_sum,
    z_out,
    z_in,
    bias_own,
    bias_pair,
    bias_mid,
    bias_dp,
    bias_last,
    bias_z,
    hidden_ref,
    enc_ref,
    gain_ref,
    shift_ref,
    bias_ref,
    counts_ref,
    offsets_ref,
    owners_ref,
    dropped_ref,
    send_sem,
    recv_sem,
    load_sem,
):
    f32, bf16 = jnp.float32, jnp.bfloat16
    n_z = n_seq // 2
    tok_rows, depth = hidden_ref.shape
    rows, out_width = weight_hbm.shape
    enc_cap = enc_ref.shape[0]
    spill_len = to_next.shape[0]
    images = counts_ref.shape[1]
    dp = lax.axis_index("dp")
    seq = lax.axis_index("seq")
    z, core = seq // 2, seq % 2
    mate_seq = z * 2 + 1 - core
    mate = (dp, mate_seq)
    used = []

    def copy(src, dst, device):
        slot = len(used)
        used.append(slot)
        return pltpu.make_async_remote_copy(
            src_ref=src,
            dst_ref=dst,
            send_sem=send_sem.at[slot],
            recv_sem=recv_sem.at[slot],
            device_id=device,
            device_id_type=pl.DeviceIdType.MESH,
        )

    square = n_dp == 4

    def dp_at(k):
        if square:
            k = abs(k)
            across_x = 1 - 2 * lax.rem(dp, 2)
            across_y = 2 - 4 * (dp // 2)
            return dp + (across_x if k % 2 else 0) + (across_y if k // 2 else 0)
        return lax.rem(dp + (k + n_dp), n_dp)

    def z_at(k):
        return lax.rem(z + (k + n_z), n_z)

    def layer_rows(dp_index, z_index, core_index):
        start = ((dp_index * n_z + z_index) * 2 + core_index) * rows
        return layer.at[pl.ds(pl.multiple_of(start, rows), rows)]

    barrier = pltpu.get_barrier_semaphore()
    for k in range(1, n_seq):
        pl.semaphore_signal(
            barrier,
            inc=1,
            device_id=(dp, lax.rem(seq + k, n_seq)),
            device_id_type=pl.DeviceIdType.MESH,
        )
    for k in range(1, n_dp):
        pl.semaphore_signal(
            barrier, inc=1, device_id=(dp_at(k), seq), device_id_type=pl.DeviceIdType.MESH
        )
    own_rows = layer_rows(dp, z, core)
    loads = []
    for src, dst in (
        (weight_hbm, own_rows),
        (enc_hbm, enc_ref),
        (gain_hbm, gain_ref),
        (shift_hbm, shift_ref),
        (counts_hbm, counts_ref),
        (offsets_hbm, offsets_ref),
        (owners_hbm, owners_ref),
        (dropped_hbm, dropped_ref),
        (hidden_hbm, hidden_ref),
        (bias_hbm, bias_ref),
    ):
        loads.append(pltpu.make_async_copy(src, dst, load_sem.at[len(loads)]))
        loads[-1].start()
    loads[0].wait()
    pl.semaphore_wait(barrier, n_seq + n_dp - 2)

    in_flight = []

    def start(src, dst, device):
        one = copy(src, dst, device)
        one.start()
        in_flight.append(one)
        return one

    direct = (1, 2) if square else range(1, n_dp)
    z_copies = {}
    dp_copies = {}
    mate_copies = []

    def spread(kz):
        block = layer_rows(dp, z_at(-kz), core)
        for k in direct:
            dp_copies[kz, k] = start(block, block, (dp_at(k), seq))
        mate_copies.append(start(block, block, mate))

    for kz in range(1, n_z):
        z_copies[kz] = start(own_rows, own_rows, (dp, z_at(kz) * 2 + core))
    spread(0)

    for one in loads[1:]:
        one.wait()
    gain = gain_ref[...][None, :]
    shift = shift_ref[...][None, :]
    step = 32 if enc_cap % 32 == 0 else enc_cap

    def norm_step(i, carry):
        at = pl.ds(pl.multiple_of(i * step, step), step)
        source[at] = layer_norm(enc_ref[at], gain, shift)[:, :out_width]
        return carry

    lax.fori_loop(0, enc_cap // step, norm_step, 0)

    count = counts_ref[...].astype(f32)
    first = offsets_ref[...].astype(f32)
    owner = owners_ref[...].astype(f32)
    drop = dropped_ref[...].astype(f32)
    down = lax.broadcasted_iota(jnp.int32, (images, images), 0)
    across = lax.broadcasted_iota(jnp.int32, (images, images), 1)

    def as_column(row):
        return jnp.sum(jnp.where(down == across, row, 0.0), axis=1, keepdims=True)

    earlier = (as_column(owner) == owner) & (down < across)
    base = jnp.sum(jnp.where(earlier, as_column(count), 0.0), axis=0, keepdims=True)

    def inside_of(shard, row_total):
        places = (
            shard * tok_rows + lax.broadcasted_iota(jnp.int32, (row_total, 1), 0)
        ).astype(f32)
        return places, (places >= first) & (places < first + count)

    def select(shard, row_total):
        places, inside = inside_of(shard, row_total)
        from_here = inside & (owner == seq.astype(f32))
        row_index = jnp.sum(
            jnp.where(from_here, base - first + places + 1.0, 0.0), axis=1, keepdims=True
        )
        lanes = lax.broadcasted_iota(jnp.int32, (row_total, enc_cap), 1).astype(f32)
        chosen = jnp.where(lanes + 1.0 == row_index, 1.0, 0.0).astype(bf16)
        return jnp.dot(chosen, source[...], preferred_element_type=f32)

    to_prev[...] = select(seq - 1, tok_rows).astype(bf16)
    prev_copy = copy(to_prev, from_next, (dp, jnp.maximum(seq - 1, 0)))

    @pl.when(seq > 0)
    def _():
        prev_copy.start()

    to_next[...] = select(seq + 1, spill_len).astype(bf16)
    next_copy = copy(to_next, from_prev, (dp, jnp.minimum(seq + 1, n_seq - 1)))

    @pl.when(seq < n_seq - 1)
    def _():
        next_copy.start()

    for kz in range(1, n_z):
        z_copies[kz].wait_recv()
        spread(kz)

    target[...] = select(seq, tok_rows)
    hidden_t[...] = hidden_ref[...].T

    for kz in range(n_z):
        for k in direct:
            dp_copies[kz, k].wait_recv()
            block = layer_rows(dp_at(-k), z_at(-kz), core)
            if square and k == 1 + kz % 2:
                dp_copies[kz, 3] = start(block, block, (dp_at(3 - k), seq))
            mate_copies.append(start(block, block, mate))
    if square:
        for kz in range(n_z):
            dp_copies[kz, 3].wait_recv()
            block = layer_rows(dp_at(3), z_at(-kz), core)
            mate_copies.append(start(block, block, mate))

    @pl.when(seq < n_seq - 1)
    def _():
        prev_copy.wait_recv()
        target[...] += from_next[...].astype(f32)

    @pl.when(seq > 0)
    def _():
        next_copy.wait_recv()
        target[:spill_len] += from_prev[...].astype(f32)

    for one in mate_copies:
        one.wait_recv()

    _, inside = inside_of(seq, tok_rows)
    count_tok = jnp.sum(jnp.where(inside, count, 0.0), axis=1, keepdims=True)
    drop_tok = jnp.sum(jnp.where(inside, drop, 0.0), axis=1, keepdims=True)
    weight_tok = jnp.where(drop_tok == 1.0, DROP_WEIGHT, 1.0) / count_tok
    projected = jnp.dot(hidden_ref[...], layer[...], preferred_element_type=f32) + bias_ref[...][None, :]
    widened = target[...]
    inv_proj = lax.rsqrt(jnp.sum(projected * projected, axis=1, keepdims=True) + LENGTH_EPS)
    inv_target = lax.rsqrt(jnp.sum(widened * widened, axis=1, keepdims=True) + LENGTH_EPS)
    cosine = jnp.sum(projected * widened, axis=1, keepdims=True) * inv_proj * inv_target
    factor = -LOSS_SCALE * weight_tok
    grad_proj[...] = (
        factor * (widened * inv_proj * inv_target - cosine * projected * inv_proj * inv_proj)
    ).astype(bf16)

    bias_own[...] = jnp.sum(grad_proj[...].astype(f32), axis=0, keepdims=True)
    bias_mate = start(bias_own, bias_pair, mate)

    chunk = depth // n_dp

    def partial_step(i, carry):
        at = pl.ds(pl.multiple_of(i * chunk, chunk), chunk)
        partial[at] = jnp.dot(hidden_t[at], grad_proj[...], preferred_element_type=f32)
        return carry

    lax.fori_loop(0, n_dp, partial_step, 0)

    def partial_rows(dp_index, z_index, core_index):
        begin = ((dp_index * n_z + z_index) * 2 + core_index) * rows
        return partial[pl.ds(pl.multiple_of(begin, rows), rows)]

    order = list(range(1, n_z)) + [0]
    pair_copies = {}
    for kz in order:
        for k in range(n_dp):
            pair_out[kz, k] = partial_rows(dp_at(k), z_at(kz), 1 - core).astype(bf16)
        pair_copies[kz] = start(pair_out.at[kz], pair_in.at[kz], mate)

    bias_mate.wait_recv()
    bias_mid[...] = bias_own[...] + bias_pair[...]
    bias_dp[pl.ds(dp, 1)] = bias_mid[...][None]
    bias_dp_copies = [
        start(bias_mid, bias_dp.at[dp], (dp_at(k), seq)) for k in range(1, n_dp)
    ]

    sum_copies = {}
    for kz in order:
        pair_copies[kz].wait_recv()
        for k in range(1, n_dp):
            total = partial_rows(dp_at(k), z_at(kz), core) + pair_in[kz, k].astype(f32)
            dp_out[kz, k - 1] = total.astype(bf16)
            sum_copies[kz, k] = start(
                dp_out.at[kz, k - 1], dp_in.at[kz, k - 1], (dp_at(k), seq)
            )
        own_sum[kz] = partial_rows(dp, z_at(kz), core) + pair_in[kz, 0].astype(f32)

    for one in bias_dp_copies:
        one.wait_recv()
    summed = bias_dp[0]
    for k in range(1, n_dp):
        summed += bias_dp[k]
    bias_last[...] = summed
    bias_z[pl.ds(z, 1)] = summed[None]
    bias_z_copies = [
        start(bias_last, bias_z.at[z], (dp, z_at(kz) * 2 + core)) for kz in range(1, n_z)
    ]

    grad_hidden_ref[...] = lax.dot_general(
        grad_proj[...], layer[...], (((1,), (1,)), ((), ())), preferred_element_type=f32
    ).astype(bf16)

    last_copies = []
    for kz in order:
        total = own_sum[kz]
        for k in range(1, n_dp):
            sum_copies[kz, k].wait_recv()
            total += dp_in[kz, k - 1].astype(f32)
        if kz:
            z_out[kz - 1] = total.astype(bf16)
            last_copies.append(
                start(z_out.at[kz - 1], z_in.at[kz - 1], (dp, z_at(kz) * 2 + core))
            )
        else:
            own_sum[0] = total

    for one in bias_z_copies:
        one.wait_recv()
    summed = bias_z[0]
    for kz in range(1, n_z):
        summed += bias_z[kz]
    grad_bias_ref[...] = summed

    total = own_sum[0]
    for at, one in enumerate(last_copies):
        one.wait_recv()
        total += z_in[at].astype(f32)
    grad_weight_ref[...] = total

    for one in in_flight:
        one.wait_send()

    @pl.when(seq > 0)
    def _():
        prev_copy.wait_send()

    @pl.when(seq < n_seq - 1)
    def _():
        next_copy.wait_send()


def fused_body(
    hidden_u,
    enc_rows,
    enc_gain,
    enc_shift,
    proj_weight,
    proj_bias,
    counts,
    offsets,
    owners,
    dropped,
    segments,
):
    n_dp, n_seq = lax.axis_size("dp"), lax.axis_size("seq")
    n_z = n_seq // 2
    tok_rows, depth = hidden_u.shape
    rows, out_width = proj_weight.shape
    enc_cap = enc_rows.shape[0]
    spill_len = tok_rows // 2
    f32, bf16 = jnp.float32, jnp.bfloat16
    copies = 3 * n_z * n_dp + 2 * n_z + n_z * n_dp + 4 * n_z + 2 * n_dp + 8
    vmem = pl.BlockSpec(memory_space=pltpu.VMEM)
    grad_hidden, grad_weight, grad_bias = pl.pallas_call(
        functools.partial(fused_kernel, n_dp, n_seq),
        out_shape=(
            jax.ShapeDtypeStruct((tok_rows, depth), bf16),
            jax.ShapeDtypeStruct((rows, out_width), f32),
            jax.ShapeDtypeStruct((1, out_width), f32),
        ),
        in_specs=[pl.BlockSpec(memory_space=pltpu.HBM)] * 10,
        out_specs=(vmem, vmem, vmem),
        scratch_shapes=[
            pltpu.VMEM((depth, out_width), bf16),
            pltpu.VMEM((enc_cap, out_width), bf16),
            pltpu.VMEM((depth, tok_rows), bf16),
            pltpu.VMEM((tok_rows, out_width), bf16),
            pltpu.VMEM((spill_len, out_width), bf16),
            pltpu.VMEM((tok_rows, out_width), bf16),
            pltpu.VMEM((spill_len, out_width), bf16),
            pltpu.VMEM((tok_rows, out_width), f32),
            pltpu.VMEM((tok_rows, out_width), bf16),
            pltpu.VMEM((depth, out_width), f32),
            pltpu.VMEM((n_z, n_dp, rows, out_width), bf16),
            pltpu.VMEM((n_z, n_dp, rows, out_width), bf16),
            pltpu.VMEM((n_z, n_dp - 1, rows, out_width), bf16),
            pltpu.VMEM((n_z, n_dp - 1, rows, out_width), bf16),
            pltpu.VMEM((n_z, rows, out_width), f32),
            pltpu.VMEM((n_z - 1, rows, out_width), bf16),
            pltpu.VMEM((n_z - 1, rows, out_width), bf16),
            pltpu.VMEM((1, out_width), f32),
            pltpu.VMEM((1, out_width), f32),
            pltpu.VMEM((1, out_width), f32),
            pltpu.VMEM((n_dp, 1, out_width), f32),
            pltpu.VMEM((1, out_width), f32),
            pltpu.VMEM((n_z, 1, out_width), f32),
            pltpu.VMEM(hidden_u.shape, bf16),
            pltpu.VMEM(enc_rows.shape, bf16),
            pltpu.VMEM(enc_gain.shape, f32),
            pltpu.VMEM(enc_shift.shape, f32),
            pltpu.VMEM(proj_bias.shape, f32),
            pltpu.VMEM(counts.shape, jnp.int32),
            pltpu.VMEM(offsets.shape, jnp.int32),
            pltpu.VMEM(owners.shape, jnp.int32),
            pltpu.VMEM(dropped.shape, jnp.int32),
            pltpu.SemaphoreType.DMA((copies,)),
            pltpu.SemaphoreType.DMA((copies,)),
            pltpu.SemaphoreType.DMA((10,)),
        ],
        compiler_params=pltpu.CompilerParams(
            collective_id=0, has_side_effects=True, vmem_limit_bytes=60 * 1024 * 1024
        ),
    )(
        hidden_u,
        enc_rows,
        enc_gain,
        enc_shift,
        proj_weight,
        proj_bias,
        counts,
        offsets,
        owners,
        dropped,
    )
    return grad_hidden, grad_weight, grad_bias[0]


def either(*arrays):
    rows, tokens = arrays[4].shape[0], arrays[0].shape[0]
    n_dp, n_seq = lax.axis_size("dp"), lax.axis_size("seq")
    whole_tiles = rows % 16 == 0 and tokens % 32 == 0
    if whole_tiles and n_seq % 2 == 0 and n_seq >= 4 and n_dp >= 2:
        return fused_body(*arrays)
    return body(*arrays)


def solution(mesh):
    placed = (
        P(("dp", "seq"), None),
        P(("dp", "seq"), None),
        P(),
        P(),
        P(("dp", "seq"), None),
        P(),
        P("dp", None),
        P("dp", None),
        P("dp", None),
        P("dp", None),
        P(("dp", "seq")),
    )
    return jax.shard_map(
        either,
        mesh=mesh,
        in_specs=placed,
        out_specs=(P(("dp", "seq"), None), P(("dp", "seq"), None), P()),
        check_vma=False,
    )
```

```python
import functools

import jax
import jax.numpy as jnp
from jax import lax
from jax.experimental import pallas as pl
from jax.experimental.pallas import tpu as pltpu
from jax.sharding import PartitionSpec as P

NORM_EPS = 1e-06
LENGTH_EPS = 1e-06
LOSS_SCALE = 1024.0
DROP_WEIGHT = 0.5


def passed_along(value, axis, steps):
    count = lax.axis_size(axis)
    first, last = (max(0, -steps), min(count, count - steps))
    return lax.ppermute(value, axis, [(source, source + steps) for source in range(first, last)])


def layer_norm(values, enc_gain, enc_shift):
    widened = values.astype(jnp.float32)
    center = widened - jnp.mean(widened, axis=-1, keepdims=True)
    spread = jnp.mean(center * center, axis=-1, keepdims=True)
    return (center * lax.rsqrt(spread + NORM_EPS) * enc_gain + enc_shift).astype(jnp.bfloat16)


def align_grad(projected, target, weight_tok):
    widened = target.astype(jnp.float32)
    inv_proj = lax.rsqrt(jnp.sum(projected * projected, axis=1, keepdims=True) + LENGTH_EPS)
    inv_target = lax.rsqrt(jnp.sum(widened * widened, axis=1, keepdims=True) + LENGTH_EPS)
    cosine = jnp.sum(projected * widened, axis=1, keepdims=True) * inv_proj * inv_target
    factor = -LOSS_SCALE * weight_tok[:, None]
    return (
        factor * (widened * inv_proj * inv_target - cosine * projected * inv_proj * inv_proj)
    ).astype(jnp.bfloat16)


def body(
    hidden_u,
    enc_rows,
    enc_gain,
    enc_shift,
    proj_weight,
    proj_bias,
    counts,
    offsets,
    owners,
    dropped,
    segments,
):
    tok_rows = hidden_u.shape[0]
    spill_len = tok_rows // 2
    out_width = proj_weight.shape[1]
    seq_index = lax.axis_index("seq")
    image_count = counts[0]
    image_start = offsets[0]
    image_owner = owners[0]
    image_drop = dropped[0]
    images = image_count.shape[0]
    index = jnp.arange(images, dtype=jnp.int32)
    earlier = (image_owner[:, None] == image_owner[None, :]) & (index[None, :] < index[:, None])
    base_row = jnp.sum(jnp.where(earlier, image_count[None, :], 0), axis=1)
    source = layer_norm(enc_rows, enc_gain, enc_shift)[:, :out_width]

    def select(target_shard, row_total):
        places = target_shard * tok_rows + jnp.arange(row_total, dtype=jnp.int32)
        inside = (places[:, None] >= image_start[None, :]) & (
            places[:, None] < (image_start + image_count)[None, :]
        )
        from_here = inside & (image_owner == seq_index)[None, :]
        row_index = jnp.sum(
            jnp.where(from_here, (base_row - image_start)[None, :] + places[:, None], 0), axis=1
        )
        present = jnp.any(from_here, axis=1)
        picked = jnp.take(source, jnp.clip(row_index, 0, source.shape[0] - 1), axis=0)
        return jnp.where(present[:, None], picked, jnp.zeros_like(picked))

    from_next = passed_along(select(seq_index - 1, tok_rows), "seq", -1)
    from_previous = passed_along(select(seq_index + 1, spill_len), "seq", 1)
    padded_spill = jnp.concatenate(
        [
            from_previous,
            jnp.zeros((tok_rows - spill_len, from_previous.shape[1]), from_previous.dtype),
        ],
        axis=0,
    )
    target = from_next + select(seq_index, tok_rows) + padded_spill
    same_image = segments[:, None] == index[None, :]
    count_tok = jnp.sum(jnp.where(same_image, image_count[None, :], 0), axis=1).astype(jnp.float32)
    drop_tok = jnp.sum(jnp.where(same_image, image_drop[None, :], 0), axis=1)
    weight_tok = jnp.where(drop_tok == 1, DROP_WEIGHT, 1.0) / count_tok
    group_weight = lax.all_gather(proj_weight, "seq", axis=0, tiled=True)
    columns = hidden_u
    projected = (
        jnp.dot(
            columns,
            lax.all_gather(group_weight, "dp", axis=0, tiled=True),
            preferred_element_type=jnp.float32,
        )
        + proj_bias
    )
    grad_proj = align_grad(projected, target, weight_tok)
    grad_hidden = lax.dot_general(
        grad_proj,
        lax.all_gather(group_weight, "dp", axis=0, tiled=True),
        (((1,), (1,)), ((), ())),
        preferred_element_type=jnp.float32,
    ).astype(jnp.bfloat16)
    columns = hidden_u
    group_grad = lax.psum_scatter(
        lax.dot_general(
            columns, grad_proj, (((0,), (0,)), ((), ())), preferred_element_type=jnp.float32
        ),
        "dp",
        scatter_dimension=0,
        tiled=True,
    )
    grad_weight = lax.psum_scatter(group_grad, "seq", scatter_dimension=0, tiled=True)
    grad_bias = lax.psum(jnp.sum(grad_proj, axis=0, dtype=jnp.float32), ("dp", "seq"))
    return (grad_hidden, grad_weight, grad_bias)


def fused_kernel(
    n_dp,
    n_seq,
    hidden_hbm,
    enc_hbm,
    gain_hbm,
    shift_hbm,
    weight_hbm,
    bias_hbm,
    counts_hbm,
    offsets_hbm,
    owners_hbm,
    dropped_hbm,
    grad_hidden_ref,
    grad_weight_ref,
    grad_bias_ref,
    layer,
    source,
    hidden_t,
    to_prev,
    to_next,
    from_next,
    from_prev,
    target,
    grad_proj,
    partial,
    pair_out,
    pair_in,
    dp_out,
    dp_in,
    own_sum,
    z_out,
    z_in,
    bias_own,
    bias_pair,
    bias_mid,
    bias_dp,
    bias_last,
    bias_z,
    hidden_ref,
    enc_ref,
    gain_ref,
    shift_ref,
    bias_ref,
    counts_ref,
    offsets_ref,
    owners_ref,
    dropped_ref,
    send_sem,
    recv_sem,
    load_sem,
):
    f32, bf16 = jnp.float32, jnp.bfloat16
    n_z = n_seq // 2
    tok_rows, depth = hidden_ref.shape
    rows, out_width = weight_hbm.shape
    enc_cap = enc_ref.shape[0]
    spill_len = to_next.shape[0]
    images = counts_ref.shape[1]
    dp = lax.axis_index("dp")
    seq = lax.axis_index("seq")
    z, core = seq // 2, seq % 2
    mate_seq = z * 2 + 1 - core
    mate = (dp, mate_seq)
    used = []

    def copy(src, dst, device):
        slot = len(used)
        used.append(slot)
        return pltpu.make_async_remote_copy(
            src_ref=src,
            dst_ref=dst,
            send_sem=send_sem.at[slot],
            recv_sem=recv_sem.at[slot],
            device_id=device,
            device_id_type=pl.DeviceIdType.MESH,
        )

    square = n_dp == 4

    def dp_at(k):
        if square:
            k = abs(k)
            across_x = 1 - 2 * lax.rem(dp, 2)
            across_y = 2 - 4 * (dp // 2)
            return dp + (across_x if k % 2 else 0) + (across_y if k // 2 else 0)
        return lax.rem(dp + (k + n_dp), n_dp)

    def z_at(k):
        return lax.rem(z + (k + n_z), n_z)

    def layer_rows(dp_index, z_index, core_index):
        start = ((dp_index * n_z + z_index) * 2 + core_index) * rows
        return layer.at[pl.ds(pl.multiple_of(start, rows), rows)]

    barrier = pltpu.get_barrier_semaphore()
    for k in range(1, n_seq):
        pl.semaphore_signal(
            barrier,
            inc=1,
            device_id=(dp, lax.rem(seq + k, n_seq)),
            device_id_type=pl.DeviceIdType.MESH,
        )
    for k in range(1, n_dp):
        pl.semaphore_signal(
            barrier, inc=1, device_id=(dp_at(k), seq), device_id_type=pl.DeviceIdType.MESH
        )
    own_rows = layer_rows(dp, z, core)
    loads = []
    for src, dst in (
        (weight_hbm, own_rows),
        (enc_hbm, enc_ref),
        (gain_hbm, gain_ref),
        (shift_hbm, shift_ref),
        (counts_hbm, counts_ref),
        (offsets_hbm, offsets_ref),
        (owners_hbm, owners_ref),
        (dropped_hbm, dropped_ref),
        (hidden_hbm, hidden_ref),
        (bias_hbm, bias_ref),
    ):
        loads.append(pltpu.make_async_copy(src, dst, load_sem.at[len(loads)]))
        loads[-1].start()
    loads[0].wait()
    pl.semaphore_wait(barrier, n_seq + n_dp - 2)

    in_flight = []

    def start(src, dst, device):
        one = copy(src, dst, device)
        one.start()
        in_flight.append(one)
        return one

    direct = (1, 2) if square else range(1, n_dp)
    z_copies = {}
    dp_copies = {}
    mate_copies = []

    def spread(kz):
        block = layer_rows(dp, z_at(-kz), core)
        for k in direct:
            dp_copies[kz, k] = start(block, block, (dp_at(k), seq))
        mate_copies.append(start(block, block, mate))

    for kz in range(1, n_z):
        z_copies[kz] = start(own_rows, own_rows, (dp, z_at(kz) * 2 + core))
    spread(0)

    for one in loads[1:]:
        one.wait()
    gain = gain_ref[...][None, :]
    shift = shift_ref[...][None, :]
    step = 32 if enc_cap % 32 == 0 else enc_cap

    def norm_step(i, carry):
        at = pl.ds(pl.multiple_of(i * step, step), step)
        source[at] = layer_norm(enc_ref[at], gain, shift)[:, :out_width]
        return carry

    lax.fori_loop(0, enc_cap // step, norm_step, 0)

    count = counts_ref[...].astype(f32)
    first = offsets_ref[...].astype(f32)
    owner = owners_ref[...].astype(f32)
    drop = dropped_ref[...].astype(f32)
    down = lax.broadcasted_iota(jnp.int32, (images, images), 0)
    across = lax.broadcasted_iota(jnp.int32, (images, images), 1)

    def as_column(row):
        return jnp.sum(jnp.where(down == across, row, 0.0), axis=1, keepdims=True)

    earlier = (as_column(owner) == owner) & (down < across)
    base = jnp.sum(jnp.where(earlier, as_column(count), 0.0), axis=0, keepdims=True)

    def inside_of(shard, row_total):
        places = (
            shard * tok_rows + lax.broadcasted_iota(jnp.int32, (row_total, 1), 0)
        ).astype(f32)
        return places, (places >= first) & (places < first + count)

    def select(shard, row_total):
        places, inside = inside_of(shard, row_total)
        from_here = inside & (owner == seq.astype(f32))
        row_index = jnp.sum(
            jnp.where(from_here, base - first + places + 1.0, 0.0), axis=1, keepdims=True
        )
        lanes = lax.broadcasted_iota(jnp.int32, (row_total, enc_cap), 1).astype(f32)
        chosen = jnp.where(lanes + 1.0 == row_index, 1.0, 0.0).astype(bf16)
        return jnp.dot(chosen, source[...], preferred_element_type=f32)

    to_prev[...] = select(seq - 1, tok_rows).astype(bf16)
    prev_copy = copy(to_prev, from_next, (dp, jnp.maximum(seq - 1, 0)))

    @pl.when(seq > 0)
    def _():
        prev_copy.start()

    to_next[...] = select(seq + 1, spill_len).astype(bf16)
    next_copy = copy(to_next, from_prev, (dp, jnp.minimum(seq + 1, n_seq - 1)))

    @pl.when(seq < n_seq - 1)
    def _():
        next_copy.start()

    for kz in range(1, n_z):
        z_copies[kz].wait_recv()
        spread(kz)

    target[...] = select(seq, tok_rows)
    hidden_t[...] = hidden_ref[...].T

    for kz in range(n_z):
        for k in direct:
            dp_copies[kz, k].wait_recv()
            block = layer_rows(dp_at(-k), z_at(-kz), core)
            if square and k == 1 + kz % 2:
                dp_copies[kz, 3] = start(block, block, (dp_at(3 - k), seq))
            mate_copies.append(start(block, block, mate))
    if square:
        for kz in range(n_z):
            dp_copies[kz, 3].wait_recv()
            block = layer_rows(dp_at(3), z_at(-kz), core)
            mate_copies.append(start(block, block, mate))

    @pl.when(seq < n_seq - 1)
    def _():
        prev_copy.wait_recv()
        target[...] += from_next[...].astype(f32)

    @pl.when(seq > 0)
    def _():
        next_copy.wait_recv()
        target[:spill_len] += from_prev[...].astype(f32)

    for one in mate_copies:
        one.wait_recv()

    _, inside = inside_of(seq, tok_rows)
    count_tok = jnp.sum(jnp.where(inside, count, 0.0), axis=1, keepdims=True)
    drop_tok = jnp.sum(jnp.where(inside, drop, 0.0), axis=1, keepdims=True)
    weight_tok = jnp.where(drop_tok == 1.0, DROP_WEIGHT, 1.0) / count_tok
    projected = jnp.dot(hidden_ref[...], layer[...], preferred_element_type=f32) + bias_ref[...][None, :]
    widened = target[...]
    inv_proj = lax.rsqrt(jnp.sum(projected * projected, axis=1, keepdims=True) + LENGTH_EPS)
    inv_target = lax.rsqrt(jnp.sum(widened * widened, axis=1, keepdims=True) + LENGTH_EPS)
    cosine = jnp.sum(projected * widened, axis=1, keepdims=True) * inv_proj * inv_target
    factor = -LOSS_SCALE * weight_tok
    grad_proj[...] = (
        factor * (widened * inv_proj * inv_target - cosine * projected * inv_proj * inv_proj)
    ).astype(bf16)

    bias_own[...] = jnp.sum(grad_proj[...].astype(f32), axis=0, keepdims=True)
    bias_mate = start(bias_own, bias_pair, mate)

    chunk = depth // n_dp

    def partial_step(i, carry):
        at = pl.ds(pl.multiple_of(i * chunk, chunk), chunk)
        partial[at] = jnp.dot(hidden_t[at], grad_proj[...], preferred_element_type=f32)
        return carry

    lax.fori_loop(0, n_dp, partial_step, 0)

    def partial_rows(dp_index, z_index, core_index):
        begin = ((dp_index * n_z + z_index) * 2 + core_index) * rows
        return partial[pl.ds(pl.multiple_of(begin, rows), rows)]

    order = list(range(1, n_z)) + [0]
    pair_copies = {}
    for kz in order:
        for k in range(n_dp):
            pair_out[kz, k] = partial_rows(dp_at(k), z_at(kz), 1 - core).astype(bf16)
        pair_copies[kz] = start(pair_out.at[kz], pair_in.at[kz], mate)

    bias_mate.wait_recv()
    bias_mid[...] = bias_own[...] + bias_pair[...]
    bias_dp[pl.ds(dp, 1)] = bias_mid[...][None]
    bias_dp_copies = [
        start(bias_mid, bias_dp.at[dp], (dp_at(k), seq)) for k in range(1, n_dp)
    ]

    sum_copies = {}
    for kz in order:
        pair_copies[kz].wait_recv()
        for k in range(1, n_dp):
            total = partial_rows(dp_at(k), z_at(kz), core) + pair_in[kz, k].astype(f32)
            dp_out[kz, k - 1] = total.astype(bf16)
            sum_copies[kz, k] = start(
                dp_out.at[kz, k - 1], dp_in.at[kz, k - 1], (dp_at(k), seq)
            )
        own_sum[kz] = partial_rows(dp, z_at(kz), core) + pair_in[kz, 0].astype(f32)

    for one in bias_dp_copies:
        one.wait_recv()
    summed = bias_dp[0]
    for k in range(1, n_dp):
        summed += bias_dp[k]
    bias_last[...] = summed
    bias_z[pl.ds(z, 1)] = summed[None]
    bias_z_copies = [
        start(bias_last, bias_z.at[z], (dp, z_at(kz) * 2 + core)) for kz in range(1, n_z)
    ]

    grad_hidden_ref[...] = lax.dot_general(
        grad_proj[...], layer[...], (((1,), (1,)), ((), ())), preferred_element_type=f32
    ).astype(bf16)

    last_copies = []
    for kz in order:
        total = own_sum[kz]
        for k in range(1, n_dp):
            sum_copies[kz, k].wait_recv()
            total += dp_in[kz, k - 1].astype(f32)
        if kz:
            z_out[kz - 1] = total.astype(bf16)
            last_copies.append(
                start(z_out.at[kz - 1], z_in.at[kz - 1], (dp, z_at(kz) * 2 + core))
            )
        else:
            own_sum[0] = total

    for one in bias_z_copies:
        one.wait_recv()
    summed = bias_z[0]
    for kz in range(1, n_z):
        summed += bias_z[kz]
    grad_bias_ref[...] = summed

    total = own_sum[0]
    for at, one in enumerate(last_copies):
        one.wait_recv()
        total += z_in[at].astype(f32)
    grad_weight_ref[...] = total

    for one in in_flight:
        one.wait_send()

    @pl.when(seq > 0)
    def _():
        prev_copy.wait_send()

    @pl.when(seq < n_seq - 1)
    def _():
        next_copy.wait_send()


def fused_body(
    hidden_u,
    enc_rows,
    enc_gain,
    enc_shift,
    proj_weight,
    proj_bias,
    counts,
    offsets,
    owners,
    dropped,
    segments,
):
    n_dp, n_seq = lax.axis_size("dp"), lax.axis_size("seq")
    n_z = n_seq // 2
    tok_rows, depth = hidden_u.shape
    rows, out_width = proj_weight.shape
    enc_cap = enc_rows.shape[0]
    spill_len = tok_rows // 2
    f32, bf16 = jnp.float32, jnp.bfloat16
    copies = 3 * n_z * n_dp + 2 * n_z + n_z * n_dp + 4 * n_z + 2 * n_dp + 8
    vmem = pl.BlockSpec(memory_space=pltpu.VMEM)
    grad_hidden, grad_weight, grad_bias = pl.pallas_call(
        functools.partial(fused_kernel, n_dp, n_seq),
        out_shape=(
            pltpu.VMEM((tok_rows, depth), bf16),
            pltpu.VMEM((rows, out_width), f32),
            pltpu.VMEM((1, out_width), f32),
        ),
        in_specs=[pl.BlockSpec(memory_space=pltpu.HBM)] * 10,
        out_specs=(vmem, vmem, vmem),
        scratch_shapes=[
            pltpu.VMEM((depth, out_width), bf16),
            pltpu.VMEM((enc_cap, out_width), bf16),
            pltpu.VMEM((depth, tok_rows), bf16),
            pltpu.VMEM((tok_rows, out_width), bf16),
            pltpu.VMEM((spill_len, out_width), bf16),
            pltpu.VMEM((tok_rows, out_width), bf16),
            pltpu.VMEM((spill_len, out_width), bf16),
            pltpu.VMEM((tok_rows, out_width), f32),
            pltpu.VMEM((tok_rows, out_width), bf16),
            pltpu.VMEM((depth, out_width), f32),
            pltpu.VMEM((n_z, n_dp, rows, out_width), bf16),
            pltpu.VMEM((n_z, n_dp, rows, out_width), bf16),
            pltpu.VMEM((n_z, n_dp - 1, rows, out_width), bf16),
            pltpu.VMEM((n_z, n_dp - 1, rows, out_width), bf16),
            pltpu.VMEM((n_z, rows, out_width), f32),
            pltpu.VMEM((n_z - 1, rows, out_width), bf16),
            pltpu.VMEM((n_z - 1, rows, out_width), bf16),
            pltpu.VMEM((1, out_width), f32),
            pltpu.VMEM((1, out_width), f32),
            pltpu.VMEM((1, out_width), f32),
            pltpu.VMEM((n_dp, 1, out_width), f32),
            pltpu.VMEM((1, out_width), f32),
            pltpu.VMEM((n_z, 1, out_width), f32),
            pltpu.VMEM(hidden_u.shape, bf16),
            pltpu.VMEM(enc_rows.shape, bf16),
            pltpu.VMEM(enc_gain.shape, f32),
            pltpu.VMEM(enc_shift.shape, f32),
            pltpu.VMEM(proj_bias.shape, f32),
            pltpu.VMEM(counts.shape, jnp.int32),
            pltpu.VMEM(offsets.shape, jnp.int32),
            pltpu.VMEM(owners.shape, jnp.int32),
            pltpu.VMEM(dropped.shape, jnp.int32),
            pltpu.SemaphoreType.DMA((copies,)),
            pltpu.SemaphoreType.DMA((copies,)),
            pltpu.SemaphoreType.DMA((10,)),
        ],
        compiler_params=pltpu.CompilerParams(
            collective_id=0, has_side_effects=True, vmem_limit_bytes=54 * 1024 * 1024
        ),
    )(
        hidden_u,
        enc_rows,
        enc_gain,
        enc_shift,
        proj_weight,
        proj_bias,
        counts,
        offsets,
        owners,
        dropped,
    )
    return grad_hidden, grad_weight, grad_bias[0]


def either(*arrays):
    rows, tokens = arrays[4].shape[0], arrays[0].shape[0]
    n_dp, n_seq = lax.axis_size("dp"), lax.axis_size("seq")
    whole_tiles = rows % 16 == 0 and tokens % 32 == 0
    if whole_tiles and n_seq % 2 == 0 and n_seq >= 4 and n_dp >= 2:
        return fused_body(*arrays)
    return body(*arrays)


def solution(mesh):
    placed = (
        P(("dp", "seq"), None),
        P(("dp", "seq"), None),
        P(),
        P(),
        P(("dp", "seq"), None),
        P(),
        P("dp", None),
        P("dp", None),
        P("dp", None),
        P("dp", None),
        P(("dp", "seq")),
    )
    return jax.shard_map(
        either,
        mesh=mesh,
        in_specs=placed,
        out_specs=(P(("dp", "seq"), None), P(("dp", "seq"), None), P()),
        check_vma=False,
    )
```

```python
import functools

import jax
import jax.numpy as jnp
from jax import lax
from jax.experimental import pallas as pl
from jax.experimental.pallas import tpu as pltpu
from jax.sharding import PartitionSpec as P

NORM_EPS = 1e-06
LENGTH_EPS = 1e-06
LOSS_SCALE = 1024.0
DROP_WEIGHT = 0.5


def passed_along(value, axis, steps):
    count = lax.axis_size(axis)
    first, last = (max(0, -steps), min(count, count - steps))
    return lax.ppermute(value, axis, [(source, source + steps) for source in range(first, last)])


def layer_norm(values, enc_gain, enc_shift):
    widened = values.astype(jnp.float32)
    center = widened - jnp.mean(widened, axis=-1, keepdims=True)
    spread = jnp.mean(center * center, axis=-1, keepdims=True)
    return (center * lax.rsqrt(spread + NORM_EPS) * enc_gain + enc_shift).astype(jnp.bfloat16)


def align_grad(projected, target, weight_tok):
    widened = target.astype(jnp.float32)
    inv_proj = lax.rsqrt(jnp.sum(projected * projected, axis=1, keepdims=True) + LENGTH_EPS)
    inv_target = lax.rsqrt(jnp.sum(widened * widened, axis=1, keepdims=True) + LENGTH_EPS)
    cosine = jnp.sum(projected * widened, axis=1, keepdims=True) * inv_proj * inv_target
    factor = -LOSS_SCALE * weight_tok[:, None]
    return (
        factor * (widened * inv_proj * inv_target - cosine * projected * inv_proj * inv_proj)
    ).astype(jnp.bfloat16)


def body(
    hidden_u,
    enc_rows,
    enc_gain,
    enc_shift,
    proj_weight,
    proj_bias,
    counts,
    offsets,
    owners,
    dropped,
    segments,
):
    tok_rows = hidden_u.shape[0]
    spill_len = tok_rows // 2
    out_width = proj_weight.shape[1]
    seq_index = lax.axis_index("seq")
    image_count = counts[0]
    image_start = offsets[0]
    image_owner = owners[0]
    image_drop = dropped[0]
    images = image_count.shape[0]
    index = jnp.arange(images, dtype=jnp.int32)
    earlier = (image_owner[:, None] == image_owner[None, :]) & (index[None, :] < index[:, None])
    base_row = jnp.sum(jnp.where(earlier, image_count[None, :], 0), axis=1)
    source = layer_norm(enc_rows, enc_gain, enc_shift)[:, :out_width]

    def select(target_shard, row_total):
        places = target_shard * tok_rows + jnp.arange(row_total, dtype=jnp.int32)
        inside = (places[:, None] >= image_start[None, :]) & (
            places[:, None] < (image_start + image_count)[None, :]
        )
        from_here = inside & (image_owner == seq_index)[None, :]
        row_index = jnp.sum(
            jnp.where(from_here, (base_row - image_start)[None, :] + places[:, None], 0), axis=1
        )
        present = jnp.any(from_here, axis=1)
        picked = jnp.take(source, jnp.clip(row_index, 0, source.shape[0] - 1), axis=0)
        return jnp.where(present[:, None], picked, jnp.zeros_like(picked))

    from_next = passed_along(select(seq_index - 1, tok_rows), "seq", -1)
    from_previous = passed_along(select(seq_index + 1, spill_len), "seq", 1)
    padded_spill = jnp.concatenate(
        [
            from_previous,
            jnp.zeros((tok_rows - spill_len, from_previous.shape[1]), from_previous.dtype),
        ],
        axis=0,
    )
    target = from_next + select(seq_index, tok_rows) + padded_spill
    same_image = segments[:, None] == index[None, :]
    count_tok = jnp.sum(jnp.where(same_image, image_count[None, :], 0), axis=1).astype(jnp.float32)
    drop_tok = jnp.sum(jnp.where(same_image, image_drop[None, :], 0), axis=1)
    weight_tok = jnp.where(drop_tok == 1, DROP_WEIGHT, 1.0) / count_tok
    group_weight = lax.all_gather(proj_weight, "seq", axis=0, tiled=True)
    columns = hidden_u
    projected = (
        jnp.dot(
            columns,
            lax.all_gather(group_weight, "dp", axis=0, tiled=True),
            preferred_element_type=jnp.float32,
        )
        + proj_bias
    )
    grad_proj = align_grad(projected, target, weight_tok)
    grad_hidden = lax.dot_general(
        grad_proj,
        lax.all_gather(group_weight, "dp", axis=0, tiled=True),
        (((1,), (1,)), ((), ())),
        preferred_element_type=jnp.float32,
    ).astype(jnp.bfloat16)
    columns = hidden_u
    group_grad = lax.psum_scatter(
        lax.dot_general(
            columns, grad_proj, (((0,), (0,)), ((), ())), preferred_element_type=jnp.float32
        ),
        "dp",
        scatter_dimension=0,
        tiled=True,
    )
    grad_weight = lax.psum_scatter(group_grad, "seq", scatter_dimension=0, tiled=True)
    grad_bias = lax.psum(jnp.sum(grad_proj, axis=0, dtype=jnp.float32), ("dp", "seq"))
    return (grad_hidden, grad_weight, grad_bias)


def fused_kernel(
    n_dp,
    n_seq,
    hidden_hbm,
    enc_hbm,
    gain_hbm,
    shift_hbm,
    weight_hbm,
    bias_hbm,
    counts_hbm,
    offsets_hbm,
    owners_hbm,
    dropped_hbm,
    grad_hidden_ref,
    grad_weight_ref,
    grad_bias_ref,
    layer,
    source,
    hidden_t,
    to_prev,
    to_next,
    from_next,
    from_prev,
    target,
    grad_proj,
    partial,
    pair_out,
    pair_in,
    dp_out,
    dp_in,
    own_sum,
    z_out,
    z_in,
    bias_own,
    bias_pair,
    bias_mid,
    bias_dp,
    bias_last,
    bias_z,
    hidden_ref,
    enc_ref,
    gain_ref,
    shift_ref,
    bias_ref,
    counts_ref,
    offsets_ref,
    owners_ref,
    dropped_ref,
    hidden_z,
    side_sum,
    send_sem,
    recv_sem,
    load_sem,
):
    f32, bf16 = jnp.float32, jnp.bfloat16
    n_z = n_seq // 2
    tok_rows, depth = hidden_ref.shape
    rows, out_width = weight_hbm.shape
    enc_cap = enc_ref.shape[0]
    spill_len = to_next.shape[0]
    images = counts_ref.shape[1]
    dp = lax.axis_index("dp")
    seq = lax.axis_index("seq")
    z, core = seq // 2, seq % 2
    mate_seq = z * 2 + 1 - core
    mate = (dp, mate_seq)
    used = []

    def copy(src, dst, device):
        slot = len(used)
        used.append(slot)
        return pltpu.make_async_remote_copy(
            src_ref=src,
            dst_ref=dst,
            send_sem=send_sem.at[slot],
            recv_sem=recv_sem.at[slot],
            device_id=device,
            device_id_type=pl.DeviceIdType.MESH,
        )

    square = n_dp == 4

    def dp_at(k):
        if square:
            k = abs(k)
            across_x = 1 - 2 * lax.rem(dp, 2)
            across_y = 2 - 4 * (dp // 2)
            return dp + (across_x if k % 2 else 0) + (across_y if k // 2 else 0)
        return lax.rem(dp + (k + n_dp), n_dp)

    def z_at(k):
        return lax.rem(z + (k + n_z), n_z)

    def layer_rows(dp_index, z_index, core_index):
        start = ((dp_index * n_z + z_index) * 2 + core_index) * rows
        return layer.at[pl.ds(pl.multiple_of(start, rows), rows)]

    barrier = pltpu.get_barrier_semaphore()
    for k in range(1, n_seq):
        pl.semaphore_signal(
            barrier,
            inc=1,
            device_id=(dp, lax.rem(seq + k, n_seq)),
            device_id_type=pl.DeviceIdType.MESH,
        )
    for k in range(1, n_dp):
        pl.semaphore_signal(
            barrier, inc=1, device_id=(dp_at(k), seq), device_id_type=pl.DeviceIdType.MESH
        )
    own_rows = layer_rows(dp, z, core)
    loads = []
    for src, dst in (
        (weight_hbm, own_rows),
        (enc_hbm, enc_ref),
        (gain_hbm, gain_ref),
        (shift_hbm, shift_ref),
        (counts_hbm, counts_ref),
        (offsets_hbm, offsets_ref),
        (owners_hbm, owners_ref),
        (dropped_hbm, dropped_ref),
        (hidden_hbm, hidden_ref),
        (bias_hbm, bias_ref),
    ):
        loads.append(pltpu.make_async_copy(src, dst, load_sem.at[len(loads)]))
        loads[-1].start()
    loads[0].wait()
    pl.semaphore_wait(barrier, n_seq + n_dp - 2)

    in_flight = []

    def start(src, dst, device):
        one = copy(src, dst, device)
        one.start()
        in_flight.append(one)
        return one

    direct = (1, 2) if square else range(1, n_dp)
    z_copies = {}
    dp_copies = {}
    mate_copies = []

    def spread(kz):
        block = layer_rows(dp, z_at(-kz), core)
        for k in direct:
            dp_copies[kz, k] = start(block, block, (dp_at(k), seq))
        mate_copies.append(start(block, block, mate))

    for kz in range(1, n_z):
        z_copies[kz] = start(own_rows, own_rows, (dp, z_at(kz) * 2 + core))
    spread(0)

    for one in loads[1:]:
        one.wait()
    gain = gain_ref[...][None, :]
    shift = shift_ref[...][None, :]
    step = 32 if enc_cap % 32 == 0 else enc_cap

    def norm_step(i, carry):
        at = pl.ds(pl.multiple_of(i * step, step), step)
        source[at] = layer_norm(enc_ref[at], gain, shift)[:, :out_width]
        return carry

    norm_steps = enc_cap // step
    lax.fori_loop(0, norm_steps // 3, norm_step, 0)
    for kz in range(1, n_z):
        z_copies[kz].wait_recv()
        spread(kz)
    lax.fori_loop(norm_steps // 3, norm_steps, norm_step, 0)

    count = counts_ref[...].astype(f32)
    first = offsets_ref[...].astype(f32)
    owner = owners_ref[...].astype(f32)
    drop = dropped_ref[...].astype(f32)
    down = lax.broadcasted_iota(jnp.int32, (images, images), 0)
    across = lax.broadcasted_iota(jnp.int32, (images, images), 1)

    def as_column(row):
        return jnp.sum(jnp.where(down == across, row, 0.0), axis=1, keepdims=True)

    earlier = (as_column(owner) == owner) & (down < across)
    base = jnp.sum(jnp.where(earlier, as_column(count), 0.0), axis=0, keepdims=True)

    def inside_of(shard, row_total):
        places = (
            shard * tok_rows + lax.broadcasted_iota(jnp.int32, (row_total, 1), 0)
        ).astype(f32)
        return places, (places >= first) & (places < first + count)

    def select(shard, row_total):
        places, inside = inside_of(shard, row_total)
        from_here = inside & (owner == seq.astype(f32))
        row_index = jnp.sum(
            jnp.where(from_here, base - first + places + 1.0, 0.0), axis=1, keepdims=True
        )
        lanes = lax.broadcasted_iota(jnp.int32, (row_total, enc_cap), 1).astype(f32)
        chosen = jnp.where(lanes + 1.0 == row_index, 1.0, 0.0).astype(bf16)
        return jnp.dot(chosen, source[...], preferred_element_type=f32)

    to_prev[...] = select(seq - 1, tok_rows).astype(bf16)
    prev_copy = copy(to_prev, from_next, (dp, jnp.maximum(seq - 1, 0)))

    @pl.when(seq > 0)
    def _():
        prev_copy.start()

    to_next[...] = select(seq + 1, spill_len).astype(bf16)
    next_copy = copy(to_next, from_prev, (dp, jnp.minimum(seq + 1, n_seq - 1)))

    @pl.when(seq < n_seq - 1)
    def _():
        next_copy.start()

    for kz in range(n_z):
        for k in direct:
            dp_copies[kz, k].wait_recv()
            block = layer_rows(dp_at(-k), z_at(-kz), core)
            if square and k == 1 + kz % 2:
                dp_copies[kz, 3] = start(block, block, (dp_at(3 - k), seq))
            mate_copies.append(start(block, block, mate))
    if square:
        for kz in range(n_z):
            dp_copies[kz, 3].wait_recv()
            block = layer_rows(dp_at(3), z_at(-kz), core)
            mate_copies.append(start(block, block, mate))

    target[...] = select(seq, tok_rows)
    hidden_t[...] = hidden_ref[...].T
    for kz in range(n_z):
        for k in range(n_dp):
            begin = (dp_at(k) * n_z + z_at(kz)) * 2 * rows
            hidden_z[kz, k * 2 * rows : (k + 1) * 2 * rows] = hidden_t[
                pl.ds(pl.multiple_of(begin, rows), 2 * rows)
            ]

    @pl.when(seq < n_seq - 1)
    def _():
        prev_copy.wait_recv()
        target[...] += from_next[...].astype(f32)

    @pl.when(seq > 0)
    def _():
        next_copy.wait_recv()
        target[:spill_len] += from_prev[...].astype(f32)

    for one in mate_copies:
        one.wait_recv()

    _, inside = inside_of(seq, tok_rows)
    count_tok = jnp.sum(jnp.where(inside, count, 0.0), axis=1, keepdims=True)
    drop_tok = jnp.sum(jnp.where(inside, drop, 0.0), axis=1, keepdims=True)
    weight_tok = jnp.where(drop_tok == 1.0, DROP_WEIGHT, 1.0) / count_tok
    projected = jnp.dot(hidden_ref[...], layer[...], preferred_element_type=f32) + bias_ref[...][None, :]
    widened = target[...]
    inv_proj = lax.rsqrt(jnp.sum(projected * projected, axis=1, keepdims=True) + LENGTH_EPS)
    inv_target = lax.rsqrt(jnp.sum(widened * widened, axis=1, keepdims=True) + LENGTH_EPS)
    cosine = jnp.sum(projected * widened, axis=1, keepdims=True) * inv_proj * inv_target
    factor = -LOSS_SCALE * weight_tok
    grad_proj[...] = (
        factor * (widened * inv_proj * inv_target - cosine * projected * inv_proj * inv_proj)
    ).astype(bf16)

    bias_own[...] = jnp.sum(grad_proj[...].astype(f32), axis=0, keepdims=True)
    bias_mate = start(bias_own, bias_pair, mate)

    def partial_rows(kz, k, core_index):
        begin = (k * 2 + core_index) * rows
        return partial[kz, pl.ds(pl.multiple_of(begin, rows), rows)]

    order = list(range(1, n_z)) + [0]
    pair_copies = {}
    for kz in order:
        partial[kz] = jnp.dot(hidden_z[kz], grad_proj[...], preferred_element_type=f32)
        for k in range(n_dp):
            pair_out[kz, k] = partial_rows(kz, k, 1 - core).astype(bf16)
        pair_copies[kz] = start(pair_out.at[kz], pair_in.at[kz], mate)

    bias_mate.wait_recv()
    bias_mid[...] = bias_own[...] + bias_pair[...]
    bias_dp[pl.ds(dp, 1)] = bias_mid[...][None]
    bias_dp_copies = [
        start(bias_mid, bias_dp.at[dp], (dp_at(k), seq)) for k in range(1, n_dp)
    ]

    def pair_total(kz, k):
        return partial_rows(kz, k, core) + pair_in[kz, k].astype(f32)

    sum_copies = {}
    for kz in order:
        pair_copies[kz].wait_recv()
        if square:
            one, two = 1 + kz % 2, 2 - kz % 2
            dp_out[kz, 0] = pair_total(kz, one).astype(bf16)
            dp_out[kz, 1] = pair_total(kz, 3).astype(bf16)
            sum_copies[kz, 1] = start(
                dp_out.at[kz, pl.ds(0, 2)], dp_in.at[kz, pl.ds(0, 2)], (dp_at(one), seq)
            )
            side_sum[kz] = pair_total(kz, two)
        else:
            for k in range(1, n_dp):
                dp_out[kz, k - 1] = pair_total(kz, k).astype(bf16)
                sum_copies[kz, k] = start(
                    dp_out.at[kz, k - 1], dp_in.at[kz, k - 1], (dp_at(k), seq)
                )
        own_sum[kz] = pair_total(kz, 0)
    if square:
        for kz in order:
            sum_copies[kz, 1].wait_recv()
            dp_out[kz, 2] = (side_sum[kz] + dp_in[kz, 1].astype(f32)).astype(bf16)
            sum_copies[kz, 2] = start(
                dp_out.at[kz, 2], dp_in.at[kz, 2], (dp_at(2 - kz % 2), seq)
            )
            own_sum[kz] += dp_in[kz, 0].astype(f32)

    for one in bias_dp_copies:
        one.wait_recv()
    summed = bias_dp[0]
    for k in range(1, n_dp):
        summed += bias_dp[k]
    bias_last[...] = summed
    bias_z[pl.ds(z, 1)] = summed[None]
    bias_z_copies = [
        start(bias_last, bias_z.at[z], (dp, z_at(kz) * 2 + core)) for kz in range(1, n_z)
    ]

    grad_hidden_ref[...] = lax.dot_general(
        grad_proj[...], layer[...], (((1,), (1,)), ((), ())), preferred_element_type=f32
    ).astype(bf16)

    last_copies = []
    for kz in order:
        total = own_sum[kz]
        if square:
            sum_copies[kz, 2].wait_recv()
            total += dp_in[kz, 2].astype(f32)
        else:
            for k in range(1, n_dp):
                sum_copies[kz, k].wait_recv()
                total += dp_in[kz, k - 1].astype(f32)
        if kz:
            z_out[kz - 1] = total.astype(bf16)
            last_copies.append(
                start(z_out.at[kz - 1], z_in.at[kz - 1], (dp, z_at(kz) * 2 + core))
            )
        else:
            own_sum[0] = total

    for one in bias_z_copies:
        one.wait_recv()
    summed = bias_z[0]
    for kz in range(1, n_z):
        summed += bias_z[kz]
    grad_bias_ref[...] = summed

    total = own_sum[0]
    for at, one in enumerate(last_copies):
        one.wait_recv()
        total += z_in[at].astype(f32)
    grad_weight_ref[...] = total

    for one in in_flight:
        one.wait_send()

    @pl.when(seq > 0)
    def _():
        prev_copy.wait_send()

    @pl.when(seq < n_seq - 1)
    def _():
        next_copy.wait_send()


def fused_body(
    hidden_u,
    enc_rows,
    enc_gain,
    enc_shift,
    proj_weight,
    proj_bias,
    counts,
    offsets,
    owners,
    dropped,
    segments,
):
    n_dp, n_seq = lax.axis_size("dp"), lax.axis_size("seq")
    n_z = n_seq // 2
    tok_rows, depth = hidden_u.shape
    rows, out_width = proj_weight.shape
    enc_cap = enc_rows.shape[0]
    spill_len = tok_rows // 2
    f32, bf16 = jnp.float32, jnp.bfloat16
    copies = 3 * n_z * n_dp + 2 * n_z + n_z * n_dp + 4 * n_z + 2 * n_dp + 8
    vmem = pl.BlockSpec(memory_space=pltpu.VMEM)
    grad_hidden, grad_weight, grad_bias = pl.pallas_call(
        functools.partial(fused_kernel, n_dp, n_seq),
        out_shape=(
            pltpu.VMEM((tok_rows, depth), bf16),
            pltpu.VMEM((rows, out_width), f32),
            pltpu.VMEM((1, out_width), f32),
        ),
        in_specs=[pl.BlockSpec(memory_space=pltpu.HBM)] * 10,
        out_specs=(vmem, vmem, vmem),
        scratch_shapes=[
            pltpu.VMEM((depth, out_width), bf16),
            pltpu.VMEM((enc_cap, out_width), bf16),
            pltpu.VMEM((depth, tok_rows), bf16),
            pltpu.VMEM((tok_rows, out_width), bf16),
            pltpu.VMEM((spill_len, out_width), bf16),
            pltpu.VMEM((tok_rows, out_width), bf16),
            pltpu.VMEM((spill_len, out_width), bf16),
            pltpu.VMEM((tok_rows, out_width), f32),
            pltpu.VMEM((tok_rows, out_width), bf16),
            pltpu.VMEM((n_z, n_dp * 2 * rows, out_width), f32),
            pltpu.VMEM((n_z, n_dp, rows, out_width), bf16),
            pltpu.VMEM((n_z, n_dp, rows, out_width), bf16),
            pltpu.VMEM((n_z, n_dp - 1, rows, out_width), bf16),
            pltpu.VMEM((n_z, n_dp - 1, rows, out_width), bf16),
            pltpu.VMEM((n_z, rows, out_width), f32),
            pltpu.VMEM((n_z - 1, rows, out_width), bf16),
            pltpu.VMEM((n_z - 1, rows, out_width), bf16),
            pltpu.VMEM((1, out_width), f32),
            pltpu.VMEM((1, out_width), f32),
            pltpu.VMEM((1, out_width), f32),
            pltpu.VMEM((n_dp, 1, out_width), f32),
            pltpu.VMEM((1, out_width), f32),
            pltpu.VMEM((n_z, 1, out_width), f32),
            pltpu.VMEM(hidden_u.shape, bf16),
            pltpu.VMEM(enc_rows.shape, bf16),
            pltpu.VMEM(enc_gain.shape, f32),
            pltpu.VMEM(enc_shift.shape, f32),
            pltpu.VMEM(proj_bias.shape, f32),
            pltpu.VMEM(counts.shape, jnp.int32),
            pltpu.VMEM(offsets.shape, jnp.int32),
            pltpu.VMEM(owners.shape, jnp.int32),
            pltpu.VMEM(dropped.shape, jnp.int32),
            pltpu.VMEM((n_z, n_dp * 2 * rows, tok_rows), bf16),
            pltpu.VMEM((n_z, rows, out_width), f32),
            pltpu.SemaphoreType.DMA((copies,)),
            pltpu.SemaphoreType.DMA((copies,)),
            pltpu.SemaphoreType.DMA((10,)),
        ],
        compiler_params=pltpu.CompilerParams(
            collective_id=0, has_side_effects=True, vmem_limit_bytes=54 * 1024 * 1024
        ),
    )(
        hidden_u,
        enc_rows,
        enc_gain,
        enc_shift,
        proj_weight,
        proj_bias,
        counts,
        offsets,
        owners,
        dropped,
    )
    return grad_hidden, grad_weight, grad_bias[0]


def either(*arrays):
    rows, tokens = arrays[4].shape[0], arrays[0].shape[0]
    n_dp, n_seq = lax.axis_size("dp"), lax.axis_size("seq")
    whole_tiles = rows % 16 == 0 and tokens % 32 == 0
    if whole_tiles and n_seq % 2 == 0 and n_seq >= 4 and n_dp >= 2:
        return fused_body(*arrays)
    return body(*arrays)


def solution(mesh):
    placed = (
        P(("dp", "seq"), None),
        P(("dp", "seq"), None),
        P(),
        P(),
        P(("dp", "seq"), None),
        P(),
        P("dp", None),
        P("dp", None),
        P("dp", None),
        P("dp", None),
        P(("dp", "seq")),
    )
    return jax.shard_map(
        either,
        mesh=mesh,
        in_specs=placed,
        out_specs=(P(("dp", "seq"), None), P(("dp", "seq"), None), P()),
        check_vma=False,
    )
```
